32 devices in a mesh: gx: 2 (over x), gy: 4 (over y, core), gz: 4 (over z).
Axes of the slice: x: 2, y: 2, z: 4, core: 2. Of those that a mesh axis runs over, the one named last changes fastest.
Arguments:
- right_side: float32 [16, 64, 1024], P('gx', 'gy', 'gz'), may hold values from -6 to 6
- coefficient: float32 [16, 64, 1024], P('gx', 'gy', 'gz'), may hold values from 0.3 to 3
- agg_weight: float32 [16, 64, 1024], P('gx', 'gy', 'gz'), may hold values from 0.03 to 0.1
- coarse_factor: float32 [256, 256], P(('gx', 'gy', 'gz')), may hold values from -0.75 to 0.75
Outputs:
- pressure_update: float32 [16, 64, 1024], P('gx', 'gy', 'gz')
- coarse_solution: float32 [256], P(('gx', 'gy', 'gz'))
The draws below stay inside these ranges and needn't reach their ends.
All inputs are finite; a program needn't handle non-finite values.
Results may differ from the reference program's by a relative error of at most 0.00024.
Values sent between devices are 32-bit elements; how exact they have to be, the bound alone decides.
A program may use at most 64 MiB of HBM per device.

```python
import math
import jax
import jax.numpy as jnp
import numpy as np
from jax import lax

ORDER = 7
CHEB = 4
CPD = 8
EXP = 8
EYP = 16
NX = 16
NY = 64
NZ = 1024
AGG = 32
NC = 256
N_GX = 2
N_GY = 4
N_GZ = 4


def raised(drawn, key, source, target, blocks, factor):
    owner, partner = [(jnp.arange(drawn.shape[dim]) // (drawn.shape[dim] // blocks)).reshape([-1 if axis == dim else 1 for axis in range(drawn.ndim)]) for dim in (source, target)]
    chosen = jax.random.permutation(key, blocks)[partner]
    strong = (owner == chosen) | (owner == (partner + blocks // 2) % blocks)
    return jnp.where(strong, factor * drawn, drawn)


def steps_of(rng, dims, cuts, low, top_value):
    def one(dim, blocks):
        draws = jax.random.uniform(jax.random.fold_in(jax.random.fold_in(rng, 6), dim), (blocks,), jnp.float32, low / len(cuts), top_value / len(cuts))
        return jnp.repeat(jnp.exp(draws), dims[dim] // blocks).reshape((-1,) + (1,) * (len(dims) - dim - 1))

    gain = one(*cuts[0])
    for cut in cuts[1:]:
        gain = gain * one(*cut)
    return gain


def scatter_about(rng, dims, scale, bound, split=(), held_as=jnp.bfloat16):
    drawn = jax.random.normal(rng, dims, jnp.float32) * scale
    if len(split) > 0:
        drawn = steps_of(rng, dims, split, -0.22, 0.18) * drawn
    return jnp.clip(drawn, min=-bound, max=bound).astype(held_as)


def heavy_noise(rng, shape, scale, reach, shards, heavy, held_as=jnp.bfloat16):
    values = scale * jax.random.normal(rng, shape, jnp.float32)
    if shards:
        values = values * steps_of(rng, shape, shards, -0.22, 0.18)
    return jnp.clip(raised(values, jax.random.fold_in(rng, 3), *heavy), -reach, reach).astype(held_as)


def setup_inputs(seed: int = 0) -> dict:
    arg_keys = jax.random.split(jax.random.key(seed), 5)
    right_side = scatter_about(arg_keys[0], (NX, NY, NZ), 1.0, 6.0, ((0, 2), (1, 4), (2, 4)), jnp.float32)
    coefficient = jnp.clip(jnp.exp(math.log(3.0) - 2.3025851 * jax.random.uniform(arg_keys[1], (NX, NY, NZ), jnp.float32) ** steps_of(arg_keys[1], (NX, NY, NZ), ((0, 2), (1, 4), (2, 4)), -0.2, 0.2)), 0.3, 3.0)
    agg_weight = jnp.clip(0.03 + 0.07 * jax.random.uniform(arg_keys[2], (NX, NY, NZ), jnp.float32) ** steps_of(arg_keys[2], (NX, NY, NZ), ((0, 2), (1, 4), (2, 4)), -0.2, 0.2), 0.03, 0.1)
    coarse_factor = heavy_noise(arg_keys[3], (NC, NC), NC ** -0.5, 0.75, ((0, 32),), (0, 1, 32, 2.75), jnp.float32)
    return dict(right_side=right_side, coefficient=coefficient, agg_weight=agg_weight, coarse_factor=coarse_factor)


highest = lax.Precision.HIGHEST
eig_high = 4.0
eig_low = 0.2
gll_inner = np.array([-0.8717401485096066153, -0.5917001814331423022, -0.2092992179024788687, 0.2092992179024788687, 0.5917001814331423022, 0.8717401485096066153])


def legendre_value(nodes, degree):
    previous = nodes * 0.0 + 1.0
    current = nodes
    for step in range(1, degree):
        following = ((2.0 * step + 1.0) * nodes * current - step * previous) / (step + 1.0)
        previous = current
        current = following
    return current


def gll_tables(poly_order):
    point_count = poly_order + 1
    gll_nodes = np.concatenate([np.array([-1.0]), gll_inner, np.array([1.0])])
    at_nodes = legendre_value(gll_nodes, poly_order)
    weights = 2.0 / (poly_order * point_count * at_nodes ** 2)
    differences = gll_nodes[:, None] - gll_nodes[None, :] + np.eye(point_count)
    derivative = at_nodes[:, None] / (at_nodes[None, :] * differences) * (1.0 - np.eye(point_count))
    end_value = poly_order * point_count / 4.0
    end_row = np.concatenate([np.array([-end_value]), np.zeros(poly_order - 1), np.array([end_value])])
    derivative = derivative + np.eye(point_count) * end_row[None, :]
    return derivative, weights


def forward_parts(field, matrix, points):
    size_x, size_y, size_z = field.shape
    grad_x = jnp.einsum("ia,eajk->eijk", matrix, field.reshape(size_x // points, points, size_y, size_z), precision=highest).reshape(field.shape)
    grad_y = jnp.einsum("ja,ieak->iejk", matrix, field.reshape(size_x, size_y // points, points, size_z), precision=highest).reshape(field.shape)
    grad_z = jnp.einsum("ka,ijea->ijek", matrix, field.reshape(size_x, size_y, size_z // points, points), precision=highest).reshape(field.shape)
    return grad_x, grad_y, grad_z


def backward_sum(parts, matrix, points):
    part_x, part_y, part_z = parts
    size_x, size_y, size_z = part_x.shape
    total = jnp.einsum("ai,eajk->eijk", matrix, part_x.reshape(size_x // points, points, size_y, size_z), precision=highest).reshape(part_x.shape)
    total = total + jnp.einsum("aj,ieak->iejk", matrix, part_y.reshape(size_x, size_y // points, points, size_z), precision=highest).reshape(part_x.shape)
    total = total + jnp.einsum("ak,ijea->ijek", matrix, part_z.reshape(size_x, size_y, size_z // points, points), precision=highest).reshape(part_x.shape)
    return total


def combine(padded, axis_dim, length, points):
    own = lax.slice_in_dim(padded, 1, length + 1, axis=axis_dim)
    left = lax.slice_in_dim(padded, 0, length, axis=axis_dim)
    right = lax.slice_in_dim(padded, 2, length + 2, axis=axis_dim)
    shape_list = [1, 1, 1]
    shape_list[axis_dim] = length
    position = (jnp.arange(length, dtype=jnp.int32) % points).reshape(shape_list)
    low_mask = (position == 0).astype(jnp.float32)
    high_mask = (position == points - 1).astype(jnp.float32)
    return own + low_mask * left + high_mask * right


def assemble(field, points):
    size_x, size_y, size_z = field.shape
    padded = jnp.pad(field, 1)
    summed = combine(padded, 0, size_x, points)
    summed = combine(summed, 1, size_y, points)
    return combine(summed, 2, size_z, points)


def reference(right_side, coefficient, agg_weight, coarse_factor):
    points = ORDER + 1
    derivative, weights = gll_tables(ORDER)
    matrix = jnp.asarray(derivative).astype(jnp.float32)
    squared = matrix * matrix
    size_x, size_y, size_z = right_side.shape
    weight_x = jnp.asarray(np.tile(weights, size_x // points)).astype(jnp.float32)
    weight_y = jnp.asarray(np.tile(weights, size_y // points)).astype(jnp.float32)
    weight_z = jnp.asarray(np.tile(weights, size_z // points)).astype(jnp.float32)
    scaled = coefficient * weight_x[:, None, None] * weight_y[None, :, None] * weight_z[None, None, :]
    diagonal = assemble(backward_sum((scaled, scaled, scaled), squared, points), points)
    inverse = 1.0 / diagonal
    theta = (eig_high + eig_low) / 2.0
    delta = (eig_high - eig_low) / 2.0
    sigma = theta / delta
    residual = right_side
    direction = inverse * residual / theta
    smoothed = direction
    rho = 1.0 / sigma
    for sweep in range(CHEB):
        grads = forward_parts(direction, matrix, points)
        local = backward_sum((scaled * grads[0], scaled * grads[1], scaled * grads[2]), matrix, points)
        residual = residual - assemble(local, points)
        if sweep + 1 < CHEB:
            rho_new = 1.0 / (2.0 * sigma - rho)
            direction = rho_new * rho * direction + (2.0 * rho_new / delta) * inverse * residual
            smoothed = smoothed + direction
            rho = rho_new
    weighted = (agg_weight * residual).reshape(N_GX, EXP, N_GY, EYP, N_GZ, CPD, AGG)
    coarse_rhs = jnp.sum(weighted, axis=(1, 3, 6)).reshape(NC)
    projected = jnp.dot(coarse_rhs, coarse_factor, precision=highest)
    coarse_solution = jnp.dot(coarse_factor, projected, precision=highest)
    spread = jnp.broadcast_to(coarse_solution.reshape(N_GX, 1, N_GY, 1, N_GZ, CPD, 1), (N_GX, EXP, N_GY, EYP, N_GZ, CPD, AGG)).reshape(NX, NY, NZ)
    pressure_update = smoothed + agg_weight * spread
    return pressure_update, coarse_solution
```

```python
import functools
import itertools

import jax
import jax.numpy as jnp
import ml_dtypes
import numpy as np
from jax import lax
from jax.experimental import pallas as pl
from jax.experimental.pallas import tpu as pltpu
from jax.sharding import PartitionSpec as P

ORDER = 7
CHEB = 4
MESH = pl.DeviceIdType.MESH
eig_high = 4.0
eig_low = 0.2
gll_inner = np.array(
    [
        -0.8717401485096066,
        -0.5917001814331423,
        -0.20929921790247888,
        0.20929921790247888,
        0.5917001814331423,
        0.8717401485096066,
    ]
)


def legendre_value(nodes, degree):
    previous = nodes * 0.0 + 1.0
    current = nodes
    for step in range(1, degree):
        following = ((2.0 * step + 1.0) * nodes * current - step * previous) / (step + 1.0)
        previous = current
        current = following
    return current


def gll_tables(poly_order):
    point_count = poly_order + 1
    gll_nodes = np.concatenate([np.array([-1.0]), gll_inner, np.array([1.0])])
    at_nodes = legendre_value(gll_nodes, poly_order)
    weights = 2.0 / (poly_order * point_count * at_nodes**2)
    differences = gll_nodes[:, None] - gll_nodes[None, :] + np.eye(point_count)
    derivative = at_nodes[:, None] / (at_nodes[None, :] * differences) * (1.0 - np.eye(point_count))
    end_value = poly_order * point_count / 4.0
    end_row = np.concatenate(
        [np.array([-end_value]), np.zeros(poly_order - 1), np.array([end_value])]
    )
    derivative = derivative + np.eye(point_count) * end_row[None, :]
    return (derivative, weights)


def halves(matrix):
    full = np.asarray(matrix, np.float32)
    high = full.astype(ml_dtypes.bfloat16)
    low = (full - high.astype(np.float32)).astype(ml_dtypes.bfloat16)
    return np.stack([high, low])


def tables(size_x, size_y, size_z):
    points = ORDER + 1
    derivative, weights = gll_tables(ORDER)
    derivative = derivative.astype(np.float32)
    squared = derivative * derivative
    ex, ey, ez = size_x // points, size_y // points, size_z // points

    def along_x(m):
        return np.kron(np.kron(np.eye(ex), m), np.eye(size_y))

    def along_y(m):
        return np.kron(np.eye(size_x), np.kron(np.eye(ey), m))

    def along_z(m):
        return np.kron(np.eye(ez), m)

    forward = np.concatenate([along_x(derivative), along_y(derivative)], axis=0)
    weights = weights.astype(np.float32)
    w_xy = np.kron(np.tile(weights, ex), np.tile(weights, ey))
    quad = (w_xy[:, None] * np.tile(weights, ez)[None, :]).astype(np.float32)
    return (
        quad,
        halves(along_x(squared.T) + along_y(squared.T)),
        halves(along_z(squared)),
        halves(forward),
        halves(along_z(derivative.T)),
        halves(forward.T),
        halves(along_z(derivative)),
    )


def split(value):
    high = value.astype(jnp.bfloat16)
    low = (value - high.astype(jnp.float32)).astype(jnp.bfloat16)
    return high, low


def dot(a, b):
    return jnp.dot(a, b, preferred_element_type=jnp.float32)


def from_left(mat, value):
    high, low = split(value)
    return dot(mat[0], high) + (dot(mat[0], low) + dot(mat[1], high))


def from_right(value, mat):
    high, low = split(value)
    return dot(high, mat[0]) + (dot(low, mat[0]) + dot(high, mat[1]))


def kernel(dims, sizes, *refs):
    gx, gy, gz = dims
    sx, sy, sz = sizes
    rows = sx * sy
    inputs, (out, out_c), scratch = refs[:11], refs[11:13], refs[13:]
    held, (field, yface, zface, xr, yr, er, zr, part, got1, got2), sems = (
        scratch[:11],
        scratch[11:21],
        scratch[21:],
    )
    in_sem, send_sem, recv_sem, send1, recv1, send2, recv2 = sems
    ix, iy, iz = (lax.axis_index(a) for a in ("gx", "gy", "gz"))

    loads = [pltpu.make_async_copy(i, h, in_sem.at[k]) for k, (i, h) in enumerate(zip(inputs, held))]
    for load in loads:
        load.start()
    coef, rhs, agg, factor, quad, sq_xy, sq_z, f_xy, f_z, b_xy, b_z = held

    for buf in (xr, yr, er, zr):
        buf[...] = jnp.zeros_like(buf)

    def options(index, count):
        if count == 1:
            return [(0, None)]
        if count == 2:
            return [(0, None), (1 - 2 * index, None)]
        return [(0, None), (1, index < count - 1), (-1, index > 0)]

    def around():
        for (dx, cx), (dy, cy), (dz, cz) in itertools.product(
            options(ix, gx), options(iy, gy), options(iz, gz)
        ):
            zero = [isinstance(d, int) and d == 0 for d in (dx, dy, dz)]
            if all(zero):
                continue
            conds = [c for c in (cx, cy, cz) if c is not None]
            cond = None
            for c in conds:
                cond = c if cond is None else jnp.logical_and(cond, c)
            yield (dx, dy, dz), zero, cond

    def guarded(cond, action):
        if cond is None:
            action()
        else:
            pl.when(cond)(action)

    nxy = gx * gy
    me_xy = ix * gy + iy
    peers1 = []
    for j in range(1, nxy):
        other = lax.rem(me_xy + j, nxy)
        peers1.append((other // gy, lax.rem(other, gy), iz))
    peers2 = [(ix, iy, lax.rem(iz + j, gz)) for j in range(1, gz)]

    barrier = pltpu.get_barrier_semaphore()
    for offset, _, cond in around():
        def greet(offset=offset):
            pl.semaphore_signal(
                barrier,
                inc=1,
                device_id=(ix + offset[0], iy + offset[1], iz + offset[2]),
                device_id_type=MESH,
            )

        guarded(cond, greet)
    for peer in peers1 + peers2:
        pl.semaphore_signal(barrier, inc=1, device_id=peer, device_id_type=MESH)

    def present(index, count):
        if count <= 2:
            return count
        return 3 - (index == 0).astype(jnp.int32) - (index == count - 1).astype(jnp.int32)

    greeted = present(ix, gx) * present(iy, gy) * present(iz, gz) - 1 + len(peers1) + len(peers2)

    def message(slot, offset, zero):
        dx, dy, dz = offset
        mark = (1 - dx) * 9 + (1 - dy) * 3 + (1 - dz)
        low_x, low_y, low_z = [(1 + d) // 2 for d in offset]
        if not zero[2]:
            src = zface.at[slot, low_z]
            dst = zr.at[slot, 1 - low_z, (1 - dx) * 3 + (1 - dy)]
        elif not zero[1] and not zero[0]:
            src = yface.at[slot, low_y]
            dst = er.at[slot, (1 - low_x) * 2 + (1 - low_y)]
        elif not zero[1]:
            src = yface.at[slot, low_y]
            dst = yr.at[slot, 1 - low_y]
        else:
            src = field.at[slot, pl.ds(pl.multiple_of(low_x * (rows - sy), sy), sy)]
            dst = xr.at[slot, 1 - low_x]
        return pltpu.make_async_remote_copy(
            src_ref=src,
            dst_ref=dst,
            send_sem=send_sem.at[slot, mark],
            recv_sem=recv_sem.at[slot, mark],
            device_id=(ix + dx, iy + dy, iz + dz),
            device_id_type=MESH,
        )

    def incoming(slot, offset, zero):
        return message(slot, tuple(-d for d in offset), zero)

    row = lax.broadcasted_iota(jnp.int32, (rows, sz), 0)
    lane = lax.broadcasted_iota(jnp.int32, (rows, sz), 1)
    y_at = lax.rem(row, sy)
    y_node = lax.rem(row, 8)
    z_node = lax.rem(lane, 8)
    x_of = lax.broadcasted_iota(jnp.int32, (sx, sz), 0)
    p_lane = lax.broadcasted_iota(jnp.int32, (8, rows), 1)
    p_y = lax.rem(p_lane, sy)
    lane_half = lax.broadcasted_iota(jnp.int32, (rows, 128), 1)

    def plane(slot, side):
        def summed_x(b):
            own = zr[slot, side, 3 + b]
            low = jnp.where(p_lane < sy, pltpu.roll(zr[slot, side, b], sy, 1), 0.0)
            high = jnp.where(
                p_lane >= rows - sy, pltpu.roll(zr[slot, side, 6 + b], rows - sy, 1), 0.0
            )
            return own + low + high

        before, mine, after = summed_x(0), summed_x(1), summed_x(2)
        low = jnp.where(
            p_y == 0, pltpu.roll(before, rows - (sy - 1), 1), pltpu.roll(mine, 1, 1)
        )
        high = jnp.where(
            p_y == sy - 1, pltpu.roll(after, sy - 1, 1), pltpu.roll(mine, rows - 1, 1)
        )
        node = lax.rem(p_lane, 8)
        return mine + jnp.where(node == 0, low, 0.0) + jnp.where(node == 7, high, 0.0)

    def assemble(slot, local):
        field[slot] = local
        cube = local.reshape(sx, sy, sz)
        yface[slot, 0] = cube[:, 0, :]
        yface[slot, 1] = cube[:, sy - 1, :]
        turned = jnp.where(lane_half < 64, local[:, :128], local[:, sz - 128 :]).T
        zface[slot, 0] = turned[:8]
        zface[slot, 1] = turned[120:]
        if slot == 0:
            pl.semaphore_wait(barrier, greeted)
        for offset, zero, cond in around():
            guarded(cond, lambda: message(slot, offset, zero).start())
        for offset, zero, cond in around():
            guarded(cond, lambda: incoming(slot, offset, zero).wait_recv())
        value = jnp.concatenate(
            [local[:sy] + xr[slot, 0], local[sy : rows - sy], local[rows - sy :] + xr[slot, 1]],
            axis=0,
        )

        def y_side(side):
            face = yr[slot, side]
            face = face + jnp.where(x_of == 0, jnp.broadcast_to(er[slot, side][sx - 1 :], (sx, sz)), 0.0)
            face = face + jnp.where(x_of == sx - 1, jnp.broadcast_to(er[slot, 2 + side][:1], (sx, sz)), 0.0)
            return jnp.broadcast_to(face[:, None, :], (sx, sy, sz)).reshape(rows, sz)

        low = jnp.where(y_at == 0, y_side(0), pltpu.roll(value, 1, 0))
        high = jnp.where(y_at == sy - 1, y_side(1), pltpu.roll(value, rows - 1, 0))
        value = value + jnp.where(y_node == 0, low, 0.0) + jnp.where(y_node == 7, high, 0.0)
        z_low = plane(slot, 0)[7:]
        z_high = plane(slot, 1)[:1]
        ends = jnp.concatenate(
            [jnp.broadcast_to(z_low, (64, rows)), jnp.broadcast_to(z_high, (64, rows))], axis=0
        ).T
        ends = jnp.concatenate([ends] * (sz // 128), axis=1)
        low = jnp.where(lane == 0, ends, pltpu.roll(value, 1, 1))
        high = jnp.where(lane == sz - 1, ends, pltpu.roll(value, sz - 1, 1))
        return value + jnp.where(z_node == 0, low, 0.0) + jnp.where(z_node == 7, high, 0.0)

    def wait_load(*which):
        for k in which:
            loads[k].wait()

    wait_load(0, 4, 5, 6)
    scaled = coef[...] * quad[...]
    diagonal = assemble(0, from_left(sq_xy, scaled) + from_right(scaled, sq_z))
    inverse = 1.0 / diagonal
    wait_load(1, 7, 8, 9, 10)
    theta = (eig_high + eig_low) / 2.0
    delta = (eig_high - eig_low) / 2.0
    sigma = theta / delta
    residual = rhs[...]
    direction = inverse * residual * (1.0 / theta)
    smoothed = direction
    rho = 1.0 / sigma
    for sweep in range(CHEB):
        grads = from_left(f_xy, direction)
        grad_z = from_right(direction, f_z)
        flux = jnp.concatenate([scaled * grads[:rows], scaled * grads[rows:]], axis=0)
        local = from_left(b_xy, flux) + from_right(scaled * grad_z, b_z)
        residual = residual - assemble(sweep + 1, local)
        if sweep + 1 < CHEB:
            rho_new = 1.0 / (2.0 * sigma - rho)
            direction = rho_new * rho * direction + (2.0 * rho_new / delta) * inverse * residual
            smoothed = smoothed + direction
            rho = rho_new

    wait_load(2, 3)
    weight = agg[...]
    count, unknowns = factor.shape
    column = jnp.sum(weight * residual, axis=0, keepdims=True)
    member = lax.broadcasted_iota(jnp.int32, (count, sz), 1) // (sz // count)
    member = member == lax.broadcasted_iota(jnp.int32, (count, sz), 0)
    coarse_rhs = jnp.sum(jnp.where(member, column, 0.0), axis=1, keepdims=True)
    x_mat = factor[...]

    def exchanged(term, which, peers, got, send, recv):
        part[which] = term
        copies = [
            pltpu.make_async_remote_copy(
                src_ref=part.at[which],
                dst_ref=got.at[j],
                send_sem=send.at[j],
                recv_sem=recv.at[j],
                device_id=peer,
                device_id_type=MESH,
            )
            for j, peer in enumerate(peers)
        ]
        for copy in copies:
            copy.start()
        for j, copy in enumerate(copies):
            copy.wait_recv()
            term = term + got[j]
        return term, copies

    term = jnp.sum(coarse_rhs * x_mat, axis=0, keepdims=True)
    term, copies1 = exchanged(term, 0, peers1, got1, send1, recv1)
    term, copies2 = exchanged(term, 1, peers2, got2, send2, recv2)
    answer = jnp.sum(x_mat * term, axis=1, keepdims=True)
    spread = jnp.sum(jnp.where(member, answer, 0.0), axis=0, keepdims=True)
    out[...] = smoothed + weight * spread
    on_lane = lax.broadcasted_iota(jnp.int32, (count, 128), 1)
    on_lane = on_lane == lax.broadcasted_iota(jnp.int32, (count, 128), 0)
    out_c[...] = jnp.sum(jnp.where(on_lane, answer, 0.0), axis=0, keepdims=True)

    for slot in range(CHEB + 1):
        for offset, zero, cond in around():
            guarded(cond, lambda: message(slot, offset, zero).wait_send())
    for copy in copies1 + copies2:
        copy.wait_send()


def per_device(dims, right_side, coefficient, agg_weight, coarse_factor):
    sizes = right_side.shape
    sx, sy, sz = sizes
    rows = sx * sy
    gx, gy, gz = dims
    flat = [a.reshape(rows, sz) for a in (coefficient, right_side, agg_weight)]
    operands = flat + [coarse_factor] + [jnp.asarray(t) for t in tables(sx, sy, sz)]
    count, unknowns = coarse_factor.shape
    slots = CHEB + 1
    f32 = jnp.float32
    dma = pltpu.SemaphoreType.DMA
    n1, n2 = max(gx * gy - 1, 1), max(gz - 1, 1)
    update, answer = pl.pallas_call(
        functools.partial(kernel, dims, sizes),
        out_shape=[
            jax.ShapeDtypeStruct((rows, sz), f32),
            jax.ShapeDtypeStruct((1, 128), f32),
        ],
        in_specs=[pl.BlockSpec(memory_space=pl.ANY)] * len(operands),
        out_specs=[pl.BlockSpec(memory_space=pltpu.VMEM)] * 2,
        scratch_shapes=[pltpu.VMEM(o.shape, o.dtype) for o in operands]
        + [
            pltpu.VMEM((slots, rows, sz), f32),
            pltpu.VMEM((slots, 2, sx, sz), f32),
            pltpu.VMEM((slots, 2, 8, rows), f32),
            pltpu.VMEM((slots, 2, sy, sz), f32),
            pltpu.VMEM((slots, 2, sx, sz), f32),
            pltpu.VMEM((slots, 4, sx, sz), f32),
            pltpu.VMEM((slots, 2, 9, 8, rows), f32),
            pltpu.VMEM((2, 1, unknowns), f32),
            pltpu.VMEM((n1, 1, unknowns), f32),
            pltpu.VMEM((n2, 1, unknowns), f32),
            dma((len(operands),)),
            dma((slots, 27)),
            dma((slots, 27)),
            dma((n1,)),
            dma((n1,)),
            dma((n2,)),
            dma((n2,)),
        ],
        compiler_params=pltpu.CompilerParams(
            collective_id=0, has_side_effects=True, vmem_limit_bytes=48 * 1024 * 1024
        ),
        cost_estimate=pl.CostEstimate(
            flops=400_000_000, bytes_accessed=2_000_000, transcendentals=0
        ),
    )(*operands)
    return update.reshape(sizes), answer[0, :count]


def solution(mesh):
    dims = tuple(mesh.shape[a] for a in ("gx", "gy", "gz"))
    return jax.shard_map(
        functools.partial(per_device, dims),
        mesh=mesh,
        in_specs=(
            P("gx", "gy", "gz"),
            P("gx", "gy", "gz"),
            P("gx", "gy", "gz"),
            P(("gx", "gy", "gz"), None),
        ),
        out_specs=(P("gx", "gy", "gz"), P(("gx", "gy", "gz"))),
        check_vma=False,
    )
```

```python
import functools
import itertools

import jax
import jax.numpy as jnp
import ml_dtypes
import numpy as np
from jax import lax
from jax.experimental import pallas as pl
from jax.experimental.pallas import tpu as pltpu
from jax.sharding import PartitionSpec as P

ORDER = 7
CHEB = 4
MESH = pl.DeviceIdType.MESH
ONE_ROUND = 64
eig_high = 4.0
eig_low = 0.2
gll_inner = np.array(
    [
        -0.8717401485096066,
        -0.5917001814331423,
        -0.20929921790247888,
        0.20929921790247888,
        0.5917001814331423,
        0.8717401485096066,
    ]
)


def legendre_value(nodes, degree):
    previous = nodes * 0.0 + 1.0
    current = nodes
    for step in range(1, degree):
        following = ((2.0 * step + 1.0) * nodes * current - step * previous) / (step + 1.0)
        previous = current
        current = following
    return current


def gll_tables(poly_order):
    point_count = poly_order + 1
    gll_nodes = np.concatenate([np.array([-1.0]), gll_inner, np.array([1.0])])
    at_nodes = legendre_value(gll_nodes, poly_order)
    weights = 2.0 / (poly_order * point_count * at_nodes**2)
    differences = gll_nodes[:, None] - gll_nodes[None, :] + np.eye(point_count)
    derivative = at_nodes[:, None] / (at_nodes[None, :] * differences) * (1.0 - np.eye(point_count))
    end_value = poly_order * point_count / 4.0
    end_row = np.concatenate(
        [np.array([-end_value]), np.zeros(poly_order - 1), np.array([end_value])]
    )
    derivative = derivative + np.eye(point_count) * end_row[None, :]
    return (derivative, weights)


def halves(matrix):
    full = np.asarray(matrix, np.float32)
    high = full.astype(ml_dtypes.bfloat16)
    low = (full - high.astype(np.float32)).astype(ml_dtypes.bfloat16)
    return np.stack([high, low])


def tables(size_x, size_y, size_z):
    points = ORDER + 1
    derivative, weights = gll_tables(ORDER)
    derivative = derivative.astype(np.float32)
    squared = derivative * derivative
    ex, ey, ez = size_x // points, size_y // points, size_z // points

    def along_x(m):
        return np.kron(np.kron(np.eye(ex), m), np.eye(size_y))

    def along_y(m):
        return np.kron(np.eye(size_x), np.kron(np.eye(ey), m))

    def along_z(m):
        return np.kron(np.eye(ez), m)

    forward = np.concatenate([along_x(derivative), along_y(derivative)], axis=0)
    weights = weights.astype(np.float32)
    w_xy = np.kron(np.tile(weights, ex), np.tile(weights, ey))
    quad = (w_xy[:, None] * np.tile(weights, ez)[None, :]).astype(np.float32)
    return (
        quad,
        halves(along_x(squared.T) + along_y(squared.T)),
        halves(along_z(squared)),
        halves(forward),
        halves(along_z(derivative.T)),
        halves(forward.T),
        halves(along_z(derivative)),
    )


def split(value):
    high = value.astype(jnp.bfloat16)
    low = (value - high.astype(jnp.float32)).astype(jnp.bfloat16)
    return high, low


def dot(a, b):
    return jnp.dot(a, b, preferred_element_type=jnp.float32)


def from_left(mat, value):
    high, low = split(value)
    return dot(mat[0], high) + (dot(mat[0], low) + dot(mat[1], high))


def from_right(value, mat):
    high, low = split(value)
    return dot(high, mat[0]) + (dot(low, mat[0]) + dot(high, mat[1]))


def kernel(dims, sizes, *refs):
    gx, gy, gz = dims
    sx, sy, sz = sizes
    rows = sx * sy
    inputs, (out, out_c), scratch = refs[:11], refs[11:13], refs[13:]
    held, (field, yface, zface, xr, yr, er, zr, part, got1, got2), sems = (
        scratch[:11],
        scratch[11:21],
        scratch[21:],
    )
    in_sem, send_sem, recv_sem, send1, recv1, send2, recv2 = sems
    ix, iy, iz = (lax.axis_index(a) for a in ("gx", "gy", "gz"))

    loads = [pltpu.make_async_copy(i, h, in_sem.at[k]) for k, (i, h) in enumerate(zip(inputs, held))]
    for load in loads:
        load.start()
    coef, rhs, agg, factor, quad, sq_xy, sq_z, f_xy, f_z, b_xy, b_z = held

    for buf in (xr, yr, er, zr):
        buf[...] = jnp.zeros_like(buf)

    def options(index, count):
        if count == 1:
            return [(0, None)]
        if count == 2:
            return [(0, None), (1 - 2 * index, None)]
        return [(0, None), (1, index < count - 1), (-1, index > 0)]

    def around():
        every = itertools.product(options(ix, gx), options(iy, gy), options(iz, gz))

        def near(one):
            return sum(isinstance(d, int) and d == 0 for d, _ in one)

        for (dx, cx), (dy, cy), (dz, cz) in sorted(every, key=near):
            zero = [isinstance(d, int) and d == 0 for d in (dx, dy, dz)]
            if all(zero):
                continue
            conds = [c for c in (cx, cy, cz) if c is not None]
            cond = None
            for c in conds:
                cond = c if cond is None else jnp.logical_and(cond, c)
            yield (dx, dy, dz), zero, cond

    def guarded(cond, action):
        if cond is None:
            action()
        else:
            pl.when(cond)(action)

    nxy = gx * gy
    me_xy = ix * gy + iy
    one_round = nxy * gz <= ONE_ROUND
    peers1 = []
    if one_round:
        for j in range(1, nxy * gz):
            other = lax.rem(me_xy * gz + iz + j, nxy * gz)
            peers1.append((other // (gy * gz), lax.rem(other // gz, gy), lax.rem(other, gz)))
        peers2 = []
    else:
        for j in range(1, nxy):
            other = lax.rem(me_xy + j, nxy)
            peers1.append((other // gy, lax.rem(other, gy), iz))
        peers2 = [(ix, iy, lax.rem(iz + j, gz)) for j in range(1, gz)]

    barrier = pltpu.get_barrier_semaphore()
    for offset, _, cond in [] if one_round else around():
        def greet(offset=offset):
            pl.semaphore_signal(
                barrier,
                inc=1,
                device_id=(ix + offset[0], iy + offset[1], iz + offset[2]),
                device_id_type=MESH,
            )

        guarded(cond, greet)
    for peer in peers1 + peers2:
        pl.semaphore_signal(barrier, inc=1, device_id=peer, device_id_type=MESH)

    def present(index, count):
        if count <= 2:
            return count
        return 3 - (index == 0).astype(jnp.int32) - (index == count - 1).astype(jnp.int32)

    greeted = len(peers1) + len(peers2)
    if not one_round:
        greeted = greeted + present(ix, gx) * present(iy, gy) * present(iz, gz) - 1

    def message(slot, offset, zero):
        dx, dy, dz = offset
        mark = (1 - dx) * 9 + (1 - dy) * 3 + (1 - dz)
        low_x, low_y, low_z = [(1 + d) // 2 for d in offset]
        if not zero[2]:
            src = zface.at[slot, low_z]
            dst = zr.at[slot, 1 - low_z, (1 - dx) * 3 + (1 - dy)]
        elif not zero[1] and not zero[0]:
            src = yface.at[slot, low_y]
            dst = er.at[slot, (1 - low_x) * 2 + (1 - low_y)]
        elif not zero[1]:
            src = yface.at[slot, low_y]
            dst = yr.at[slot, 1 - low_y]
        else:
            src = field.at[slot, pl.ds(pl.multiple_of(low_x * (rows - sy), sy), sy)]
            dst = xr.at[slot, 1 - low_x]
        return pltpu.make_async_remote_copy(
            src_ref=src,
            dst_ref=dst,
            send_sem=send_sem.at[slot, mark],
            recv_sem=recv_sem.at[slot, mark],
            device_id=(ix + dx, iy + dy, iz + dz),
            device_id_type=MESH,
        )

    def incoming(slot, offset, zero):
        return message(slot, tuple(-d for d in offset), zero)

    row = lax.broadcasted_iota(jnp.int32, (rows, sz), 0)
    lane = lax.broadcasted_iota(jnp.int32, (rows, sz), 1)
    y_at = lax.rem(row, sy)
    y_node = lax.rem(row, 8)
    z_node = lax.rem(lane, 8)
    x_of = lax.broadcasted_iota(jnp.int32, (sx, sz), 0)
    p_lane = lax.broadcasted_iota(jnp.int32, (8, rows), 1)
    p_y = lax.rem(p_lane, sy)
    lane_half = lax.broadcasted_iota(jnp.int32, (rows, 128), 1)

    def plane(slot, side):
        def summed_x(b):
            own = zr[slot, side, 3 + b]
            low = jnp.where(p_lane < sy, pltpu.roll(zr[slot, side, b], sy, 1), 0.0)
            high = jnp.where(
                p_lane >= rows - sy, pltpu.roll(zr[slot, side, 6 + b], rows - sy, 1), 0.0
            )
            return own + low + high

        before, mine, after = summed_x(0), summed_x(1), summed_x(2)
        low = jnp.where(
            p_y == 0, pltpu.roll(before, rows - (sy - 1), 1), pltpu.roll(mine, 1, 1)
        )
        high = jnp.where(
            p_y == sy - 1, pltpu.roll(after, sy - 1, 1), pltpu.roll(mine, rows - 1, 1)
        )
        node = lax.rem(p_lane, 8)
        return mine + jnp.where(node == 0, low, 0.0) + jnp.where(node == 7, high, 0.0)

    def assemble(slot, local):
        field[slot] = local
        cube = local.reshape(sx, sy, sz)
        yface[slot, 0] = cube[:, 0, :]
        yface[slot, 1] = cube[:, sy - 1, :]
        turned = jnp.where(lane_half < 64, local[:, :128], local[:, sz - 128 :]).T
        zface[slot, 0] = turned[:8]
        zface[slot, 1] = turned[120:]
        if slot == 0:
            pl.semaphore_wait(barrier, greeted)
        for offset, zero, cond in around():
            guarded(cond, lambda: message(slot, offset, zero).start())
        for offset, zero, cond in around():
            guarded(cond, lambda: incoming(slot, offset, zero).wait_recv())
        value = jnp.concatenate(
            [local[:sy] + xr[slot, 0], local[sy : rows - sy], local[rows - sy :] + xr[slot, 1]],
            axis=0,
        )

        def y_side(side):
            face = yr[slot, side]
            face = face + jnp.where(x_of == 0, jnp.broadcast_to(er[slot, side][sx - 1 :], (sx, sz)), 0.0)
            face = face + jnp.where(x_of == sx - 1, jnp.broadcast_to(er[slot, 2 + side][:1], (sx, sz)), 0.0)
            return jnp.broadcast_to(face[:, None, :], (sx, sy, sz)).reshape(rows, sz)

        low = jnp.where(y_at == 0, y_side(0), pltpu.roll(value, 1, 0))
        high = jnp.where(y_at == sy - 1, y_side(1), pltpu.roll(value, rows - 1, 0))
        value = value + jnp.where(y_node == 0, low, 0.0) + jnp.where(y_node == 7, high, 0.0)
        z_low = plane(slot, 0)[7:]
        z_high = plane(slot, 1)[:1]
        ends = jnp.concatenate(
            [jnp.broadcast_to(z_low, (64, rows)), jnp.broadcast_to(z_high, (64, rows))], axis=0
        ).T
        ends = jnp.concatenate([ends] * (sz // 128), axis=1)
        low = jnp.where(lane == 0, ends, pltpu.roll(value, 1, 1))
        high = jnp.where(lane == sz - 1, ends, pltpu.roll(value, sz - 1, 1))
        return value + jnp.where(z_node == 0, low, 0.0) + jnp.where(z_node == 7, high, 0.0)

    def wait_load(*which):
        for k in which:
            loads[k].wait()

    wait_load(0, 4, 5, 6)
    scaled = coef[...] * quad[...]
    diagonal = assemble(0, from_left(sq_xy, scaled) + from_right(scaled, sq_z))
    inverse = 1.0 / diagonal
    wait_load(1, 7, 8, 9, 10)
    theta = (eig_high + eig_low) / 2.0
    delta = (eig_high - eig_low) / 2.0
    sigma = theta / delta
    residual = rhs[...]
    direction = inverse * residual * (1.0 / theta)
    smoothed = direction
    rho = 1.0 / sigma
    for sweep in range(CHEB):
        grads = from_left(f_xy, direction)
        grad_z = from_right(direction, f_z)
        flux = jnp.concatenate([scaled * grads[:rows], scaled * grads[rows:]], axis=0)
        local = from_left(b_xy, flux) + from_right(scaled * grad_z, b_z)
        residual = residual - assemble(sweep + 1, local)
        if sweep + 1 < CHEB:
            rho_new = 1.0 / (2.0 * sigma - rho)
            direction = rho_new * rho * direction + (2.0 * rho_new / delta) * inverse * residual
            smoothed = smoothed + direction
            rho = rho_new

    wait_load(2, 3)
    weight = agg[...]
    count, unknowns = factor.shape
    column = jnp.sum(weight * residual, axis=0, keepdims=True)
    member = lax.broadcasted_iota(jnp.int32, (count, sz), 1) // (sz // count)
    member = member == lax.broadcasted_iota(jnp.int32, (count, sz), 0)
    coarse_rhs = jnp.sum(jnp.where(member, column, 0.0), axis=1, keepdims=True)
    x_mat = factor[...]

    def exchanged(term, which, peers, got, send, recv):
        part[which] = term
        copies = [
            pltpu.make_async_remote_copy(
                src_ref=part.at[which],
                dst_ref=got.at[j],
                send_sem=send.at[j],
                recv_sem=recv.at[j],
                device_id=peer,
                device_id_type=MESH,
            )
            for j, peer in enumerate(peers)
        ]
        for copy in copies:
            copy.start()
        for j, copy in enumerate(copies):
            copy.wait_recv()
            term = term + got[j]
        return term, copies

    term = jnp.sum(coarse_rhs * x_mat, axis=0, keepdims=True)
    term, copies1 = exchanged(term, 0, peers1, got1, send1, recv1)
    term, copies2 = exchanged(term, 1, peers2, got2, send2, recv2)
    answer = jnp.sum(x_mat * term, axis=1, keepdims=True)
    spread = jnp.sum(jnp.where(member, answer, 0.0), axis=0, keepdims=True)
    out[...] = smoothed + weight * spread
    on_lane = lax.broadcasted_iota(jnp.int32, (count, 128), 1)
    on_lane = on_lane == lax.broadcasted_iota(jnp.int32, (count, 128), 0)
    out_c[...] = jnp.sum(jnp.where(on_lane, answer, 0.0), axis=0)[:count]

    for slot in range(CHEB + 1):
        for offset, zero, cond in around():
            guarded(cond, lambda: message(slot, offset, zero).wait_send())
    for copy in copies1 + copies2:
        copy.wait_send()


def per_device(dims, right_side, coefficient, agg_weight, coarse_factor):
    sizes = right_side.shape
    sx, sy, sz = sizes
    rows = sx * sy
    gx, gy, gz = dims
    flat = [a.reshape(rows, sz) for a in (coefficient, right_side, agg_weight)]
    operands = flat + [coarse_factor] + [jnp.asarray(t) for t in tables(sx, sy, sz)]
    count, unknowns = coarse_factor.shape
    slots = CHEB + 1
    f32 = jnp.float32
    dma = pltpu.SemaphoreType.DMA
    n1, n2 = max(gx * gy - 1, 1), max(gz - 1, 1)
    if gx * gy * gz <= ONE_ROUND:
        n1 = max(gx * gy * gz - 1, 1)
    update, answer = pl.pallas_call(
        functools.partial(kernel, dims, sizes),
        out_shape=[
            pltpu.VMEM((rows, sz), f32),
            pltpu.VMEM((count,), f32),
        ],
        in_specs=[pl.BlockSpec(memory_space=pltpu.HBM)] * len(operands),
        out_specs=[pl.BlockSpec(memory_space=pltpu.VMEM)] * 2,
        scratch_shapes=[pltpu.VMEM(o.shape, o.dtype) for o in operands]
        + [
            pltpu.VMEM((slots, rows, sz), f32),
            pltpu.VMEM((slots, 2, sx, sz), f32),
            pltpu.VMEM((slots, 2, 8, rows), f32),
            pltpu.VMEM((slots, 2, sy, sz), f32),
            pltpu.VMEM((slots, 2, sx, sz), f32),
            pltpu.VMEM((slots, 4, sx, sz), f32),
            pltpu.VMEM((slots, 2, 9, 8, rows), f32),
            pltpu.VMEM((2, 1, unknowns), f32),
            pltpu.VMEM((n1, 1, unknowns), f32),
            pltpu.VMEM((n2, 1, unknowns), f32),
            dma((len(operands),)),
            dma((slots, 27)),
            dma((slots, 27)),
            dma((n1,)),
            dma((n1,)),
            dma((n2,)),
            dma((n2,)),
        ],
        compiler_params=pltpu.CompilerParams(
            collective_id=0, has_side_effects=True, vmem_limit_bytes=63 * 1024 * 1024
        ),
        cost_estimate=pl.CostEstimate(
            flops=400_000_000, bytes_accessed=2_000_000, transcendentals=0
        ),
    )(*operands)
    return update.reshape(sizes), answer


def solution(mesh):
    dims = tuple(mesh.shape[a] for a in ("gx", "gy", "gz"))
    return jax.shard_map(
        functools.partial(per_device, dims),
        mesh=mesh,
        in_specs=(
            P("gx", "gy", "gz"),
            P("gx", "gy", "gz"),
            P("gx", "gy", "gz"),
            P(("gx", "gy", "gz"), None),
        ),
        out_specs=(P("gx", "gy", "gz"), P(("gx", "gy", "gz"))),
        check_vma=False,
    )
```

```python
import functools
import itertools

import jax
import jax.numpy as jnp
import ml_dtypes
import numpy as np
from jax import lax
from jax.experimental import pallas as pl
from jax.experimental.pallas import tpu as pltpu
from jax.sharding import PartitionSpec as P

ORDER = 7
CHEB = 4
MESH = pl.DeviceIdType.MESH
ONE_ROUND = 64
eig_high = 4.0
eig_low = 0.2
gll_inner = np.array(
    [
        -0.8717401485096066,
        -0.5917001814331423,
        -0.20929921790247888,
        0.20929921790247888,
        0.5917001814331423,
        0.8717401485096066,
    ]
)


def legendre_value(nodes, degree):
    previous = nodes * 0.0 + 1.0
    current = nodes
    for step in range(1, degree):
        following = ((2.0 * step + 1.0) * nodes * current - step * previous) / (step + 1.0)
        previous = current
        current = following
    return current


def gll_tables(poly_order):
    point_count = poly_order + 1
    gll_nodes = np.concatenate([np.array([-1.0]), gll_inner, np.array([1.0])])
    at_nodes = legendre_value(gll_nodes, poly_order)
    weights = 2.0 / (poly_order * point_count * at_nodes**2)
    differences = gll_nodes[:, None] - gll_nodes[None, :] + np.eye(point_count)
    derivative = at_nodes[:, None] / (at_nodes[None, :] * differences) * (1.0 - np.eye(point_count))
    end_value = poly_order * point_count / 4.0
    end_row = np.concatenate(
        [np.array([-end_value]), np.zeros(poly_order - 1), np.array([end_value])]
    )
    derivative = derivative + np.eye(point_count) * end_row[None, :]
    return (derivative, weights)


def halves(matrix):
    full = np.asarray(matrix, np.float32)
    high = full.astype(ml_dtypes.bfloat16)
    low = (full - high.astype(np.float32)).astype(ml_dtypes.bfloat16)
    return np.stack([high, low])


def tables(size_x, size_y, size_z):
    points = ORDER + 1
    derivative, weights = gll_tables(ORDER)
    derivative = derivative.astype(np.float32)
    squared = derivative * derivative
    ex, ey, ez = size_x // points, size_y // points, size_z // points

    def along_x(m):
        return np.kron(np.kron(np.eye(ex), m), np.eye(size_y))

    def along_y(m):
        return np.kron(np.eye(size_x), np.kron(np.eye(ey), m))

    def along_z(m):
        return np.kron(np.eye(ez), m)

    forward = np.concatenate([along_x(derivative), along_y(derivative)], axis=0)
    weights = weights.astype(np.float32)
    w_xy = np.kron(np.tile(weights, ex), np.tile(weights, ey))
    quad = (w_xy[:, None] * np.tile(weights, ez)[None, :]).astype(np.float32)
    return (
        quad,
        halves(along_x(squared.T) + along_y(squared.T)),
        halves(along_z(squared)),
        halves(forward),
        halves(along_z(derivative.T)),
        halves(forward.T),
        halves(along_z(derivative)),
    )


def split(value):
    high = value.astype(jnp.bfloat16)
    low = (value - high.astype(jnp.float32)).astype(jnp.bfloat16)
    return high, low


def dot(a, b):
    return jnp.dot(a, b, preferred_element_type=jnp.float32)


def from_left(mat, value):
    high, low = split(value)
    return dot(mat[0], high) + (dot(mat[0], low) + dot(mat[1], high))


def from_right(value, mat):
    high, low = split(value)
    return dot(high, mat[0]) + (dot(low, mat[0]) + dot(high, mat[1]))


def kernel(dims, sizes, *refs):
    gx, gy, gz = dims
    sx, sy, sz = sizes
    rows = sx * sy
    inputs, (out, out_c), scratch = refs[:11], refs[11:13], refs[13:]
    held, (field, yface, zface, xr, yr, er, zr, xn, part, got1, got2), sems = (
        scratch[:11],
        scratch[11:22],
        scratch[22:],
    )
    in_sem, send_sem, recv_sem, sendx, recvx, send1, recv1, send2, recv2 = sems
    ix, iy, iz = (lax.axis_index(a) for a in ("gx", "gy", "gz"))

    loads = [pltpu.make_async_copy(i, h, in_sem.at[k]) for k, (i, h) in enumerate(zip(inputs, held))]
    for load in loads:
        load.start()
    coef, rhs, agg, factor, quad, sq_xy, sq_z, f_xy, f_z, b_xy, b_z = held

    for buf in (xr, yr, er, zr, xn):
        buf[...] = jnp.zeros_like(buf)

    def options(index, count):
        if count == 1:
            return [(0, None)]
        if count == 2:
            return [(0, None), (1 - 2 * index, None)]
        return [(0, None), (1, index < count - 1), (-1, index > 0)]

    def around():
        every = itertools.product(options(ix, gx), options(iy, gy), options(iz, gz))

        def near(one):
            return sum(isinstance(d, int) and d == 0 for d, _ in one)

        for (dx, cx), (dy, cy), (dz, cz) in sorted(every, key=near):
            zero = [isinstance(d, int) and d == 0 for d in (dx, dy, dz)]
            if all(zero):
                continue
            conds = [c for c in (cx, cy, cz) if c is not None]
            cond = None
            for c in conds:
                cond = c if cond is None else jnp.logical_and(cond, c)
            yield (dx, dy, dz), zero, cond

    def guarded(cond, action):
        if cond is None:
            action()
        else:
            pl.when(cond)(action)

    nxy = gx * gy
    me_xy = ix * gy + iy
    one_round = nxy * gz <= ONE_ROUND
    peers1 = []
    if one_round:
        for j in range(1, nxy * gz):
            other = lax.rem(me_xy * gz + iz + j, nxy * gz)
            peers1.append((other // (gy * gz), lax.rem(other // gz, gy), lax.rem(other, gz)))
        peers2 = []
    else:
        for j in range(1, nxy):
            other = lax.rem(me_xy + j, nxy)
            peers1.append((other // gy, lax.rem(other, gy), iz))
        peers2 = [(ix, iy, lax.rem(iz + j, gz)) for j in range(1, gz)]

    barrier = pltpu.get_barrier_semaphore()
    for offset, _, cond in [] if one_round else around():
        def greet(offset=offset):
            pl.semaphore_signal(
                barrier,
                inc=1,
                device_id=(ix + offset[0], iy + offset[1], iz + offset[2]),
                device_id_type=MESH,
            )

        guarded(cond, greet)
    for peer in peers1 + peers2:
        pl.semaphore_signal(barrier, inc=1, device_id=peer, device_id_type=MESH)

    def present(index, count):
        if count <= 2:
            return count
        return 3 - (index == 0).astype(jnp.int32) - (index == count - 1).astype(jnp.int32)

    greeted = len(peers1) + len(peers2)
    if not one_round:
        greeted = greeted + present(ix, gx) * present(iy, gy) * present(iz, gz) - 1

    def message(slot, offset, zero):
        dx, dy, dz = offset
        mark = (1 - dx) * 9 + (1 - dy) * 3 + (1 - dz)
        low_x, low_y, low_z = [(1 + d) // 2 for d in offset]
        if not zero[2]:
            src = zface.at[slot, low_z]
            dst = zr.at[slot, 1 - low_z, (1 - dx) * 3 + (1 - dy)]
        elif not zero[1] and not zero[0]:
            src = yface.at[slot, low_y]
            dst = er.at[slot, (1 - low_x) * 2 + (1 - low_y)]
        elif not zero[1]:
            src = yface.at[slot, low_y]
            dst = yr.at[slot, 1 - low_y]
        else:
            src = field.at[slot, pl.ds(pl.multiple_of(low_x * (rows - sy), sy), sy)]
            dst = xr.at[slot, 1 - low_x]
        return pltpu.make_async_remote_copy(
            src_ref=src,
            dst_ref=dst,
            send_sem=send_sem.at[slot, mark],
            recv_sem=recv_sem.at[slot, mark],
            device_id=(ix + dx, iy + dy, iz + dz),
            device_id_type=MESH,
        )

    def incoming(slot, offset, zero):
        return message(slot, tuple(-d for d in offset), zero)

    def rows_message(offset):
        dx, dy, dz = offset
        mark = (1 - dx) * 9 + (1 - dy) * 3 + (1 - dz)
        return pltpu.make_async_remote_copy(
            src_ref=factor,
            dst_ref=xn.at[mark],
            send_sem=sendx.at[mark],
            recv_sem=recvx.at[mark],
            device_id=(ix + dx, iy + dy, iz + dz),
            device_id_type=MESH,
        )

    row = lax.broadcasted_iota(jnp.int32, (rows, sz), 0)
    lane = lax.broadcasted_iota(jnp.int32, (rows, sz), 1)
    y_at = lax.rem(row, sy)
    y_node = lax.rem(row, 8)
    z_node = lax.rem(lane, 8)
    x_of = lax.broadcasted_iota(jnp.int32, (sx, sz), 0)
    p_lane = lax.broadcasted_iota(jnp.int32, (8, rows), 1)
    p_y = lax.rem(p_lane, sy)
    lane_half = lax.broadcasted_iota(jnp.int32, (rows, 128), 1)

    def plane(slot, side):
        def summed_x(b):
            own = zr[slot, side, 3 + b]
            low = jnp.where(p_lane < sy, pltpu.roll(zr[slot, side, b], sy, 1), 0.0)
            high = jnp.where(
                p_lane >= rows - sy, pltpu.roll(zr[slot, side, 6 + b], rows - sy, 1), 0.0
            )
            return own + low + high

        before, mine, after = summed_x(0), summed_x(1), summed_x(2)
        low = jnp.where(
            p_y == 0, pltpu.roll(before, rows - (sy - 1), 1), pltpu.roll(mine, 1, 1)
        )
        high = jnp.where(
            p_y == sy - 1, pltpu.roll(after, sy - 1, 1), pltpu.roll(mine, rows - 1, 1)
        )
        node = lax.rem(p_lane, 8)
        return mine + jnp.where(node == 0, low, 0.0) + jnp.where(node == 7, high, 0.0)

    def end_rows(local):
        return jnp.where(lane_half < 64, local[:, :128], local[:, sz - 128 :]).T

    def publish(slot, local):
        field[slot] = local
        cube = local.reshape(sx, sy, sz)
        yface[slot, 0] = cube[:, 0, :]
        yface[slot, 1] = cube[:, sy - 1, :]
        turned = end_rows(local)
        zface[slot, 0] = turned[:8]
        zface[slot, 1] = turned[120:]
        if slot == 0:
            pl.semaphore_wait(barrier, greeted)
        for offset, zero, cond in around():
            guarded(cond, lambda: message(slot, offset, zero).start())

    def assemble(slot, local, meanwhile):
        publish(slot, local)
        meanwhile()
        for offset, zero, cond in around():
            guarded(cond, lambda: incoming(slot, offset, zero).wait_recv())
        value = jnp.concatenate(
            [local[:sy] + xr[slot, 0], local[sy : rows - sy], local[rows - sy :] + xr[slot, 1]],
            axis=0,
        )

        def y_side(side):
            face = yr[slot, side]
            face = face + jnp.where(x_of == 0, jnp.broadcast_to(er[slot, side][sx - 1 :], (sx, sz)), 0.0)
            face = face + jnp.where(x_of == sx - 1, jnp.broadcast_to(er[slot, 2 + side][:1], (sx, sz)), 0.0)
            return jnp.broadcast_to(face[:, None, :], (sx, sy, sz)).reshape(rows, sz)

        low = jnp.where(y_at == 0, y_side(0), pltpu.roll(value, 1, 0))
        high = jnp.where(y_at == sy - 1, y_side(1), pltpu.roll(value, rows - 1, 0))
        value = value + jnp.where(y_node == 0, low, 0.0) + jnp.where(y_node == 7, high, 0.0)
        z_low = plane(slot, 0)[7:]
        z_high = plane(slot, 1)[:1]
        ends = jnp.concatenate(
            [jnp.broadcast_to(z_low, (64, rows)), jnp.broadcast_to(z_high, (64, rows))], axis=0
        ).T
        ends = jnp.concatenate([ends] * (sz // 128), axis=1)
        low = jnp.where(lane == 0, ends, pltpu.roll(value, 1, 1))
        high = jnp.where(lane == sz - 1, ends, pltpu.roll(value, sz - 1, 1))
        return value + jnp.where(z_node == 0, low, 0.0) + jnp.where(z_node == 7, high, 0.0)

    def wait_load(*which):
        for k in which:
            loads[k].wait()

    def early():
        wait_load(2, 3)
        publish(CHEB, agg[...])
        for offset, zero, cond in around():
            guarded(cond, lambda: rows_message(offset).start())
        wait_load(1, 7, 8, 9, 10)

    def arrived():
        for offset, zero, cond in around():
            def both(offset=offset, zero=zero):
                incoming(CHEB, offset, zero).wait_recv()
                rows_message(tuple(-d for d in offset)).wait_recv()

            guarded(cond, both)

    wait_load(0, 4, 5, 6)
    scaled = coef[...] * quad[...]
    diagonal = assemble(0, from_left(sq_xy, scaled) + from_right(scaled, sq_z), early)
    inverse = 1.0 / diagonal
    theta = (eig_high + eig_low) / 2.0
    delta = (eig_high - eig_low) / 2.0
    sigma = theta / delta
    residual = rhs[...]
    direction = inverse * residual * (1.0 / theta)
    smoothed = direction
    rho = 1.0 / sigma
    for sweep in range(CHEB):
        grads = from_left(f_xy, direction)
        grad_z = from_right(direction, f_z)
        flux = jnp.concatenate([scaled * grads[:rows], scaled * grads[rows:]], axis=0)
        local = from_left(b_xy, flux) + from_right(scaled * grad_z, b_z)
        if sweep + 1 < CHEB:
            meanwhile = arrived if sweep + 2 == CHEB else lambda: None
            residual = residual - assemble(sweep + 1, local, meanwhile)
            rho_new = 1.0 / (2.0 * sigma - rho)
            direction = rho_new * rho * direction + (2.0 * rho_new / delta) * inverse * residual
            smoothed = smoothed + direction
            rho = rho_new

    weight = agg[...]
    count, unknowns = factor.shape
    member = lax.broadcasted_iota(jnp.int32, (count, sz), 1) // (sz // count)
    member = member == lax.broadcasted_iota(jnp.int32, (count, sz), 0)
    last = CHEB

    def per_aggregate(column):
        return jnp.sum(jnp.where(member, column, 0.0), axis=1, keepdims=True)

    def inner_y(value, at, axis):
        size = value.shape[axis]
        node = lax.rem(at, 8)
        low = jnp.where((node == 0) & (at != 0), pltpu.roll(value, 1, axis), 0.0)
        high = jnp.where((node == 7) & (at != sy - 1), pltpu.roll(value, size - 1, axis), 0.0)
        return value + low + high

    low = jnp.where((z_node == 0) & (lane != 0), pltpu.roll(local, 1, 1), 0.0)
    high = jnp.where((z_node == 7) & (lane != sz - 1), pltpu.roll(local, sz - 1, 1), 0.0)
    joined = local + low + high
    cube = joined.reshape(sx, sy, sz)
    y_ends = (cube[:, 0, :], cube[:, sy - 1, :])

    def total(value):
        return jnp.sum(value, axis=0, keepdims=True)

    terms = [
        (per_aggregate(total(weight * residual - inner_y(weight, y_at, 0) * joined)), factor[...])
    ]
    for side in range(2):
        layer = inner_y(xr[last, side], y_at[:sy], 0)
        own = joined[side * (rows - sy) : side * (rows - sy) + sy]
        terms.append((-per_aggregate(total(layer * own)), xn[side * 18 + 4]))
        terms.append((-per_aggregate(total(yr[last, side] * y_ends[side])), xn[9 + side * 6 + 1]))
        for other in range(2):
            line = er[last, side * 2 + other][(1 - side) * (sx - 1) : (1 - side) * (sx - 1) + 1]
            own = y_ends[other][side * (sx - 1) : side * (sx - 1) + 1]
            terms.append((-per_aggregate(line * own), xn[side * 18 + other * 6 + 1]))

    turned = end_rows(local)
    tile_row = lax.broadcasted_iota(jnp.int32, (8, 1), 0)
    for side in range(2):
        own = jnp.broadcast_to(turned[side * 127 : side * 127 + 1], (8, rows))
        for a, b in itertools.product(range(3), range(3)):
            face = zr[last, side, a * 3 + b]
            if a == 0:
                face = jnp.where(p_lane < sy, pltpu.roll(face, sy, 1), 0.0)
            elif a == 2:
                face = jnp.where(p_lane >= rows - sy, pltpu.roll(face, rows - sy, 1), 0.0)
            if b == 0:
                face = jnp.where(p_y == 0, pltpu.roll(face, rows - (sy - 1), 1), 0.0)
            elif b == 2:
                face = jnp.where(p_y == sy - 1, pltpu.roll(face, sy - 1, 1), 0.0)
            else:
                face = inner_y(face, p_y, 1)
            amount = jnp.sum(face * own, axis=1, keepdims=True)
            amount = jnp.where(tile_row == 7 * (1 - side), amount, 0.0)
            terms.append((-amount, xn[a * 9 + b * 3 + side * 2]))
    x_mat = factor[...]

    def exchanged(term, which, peers, got, send, recv, meanwhile):
        part[which] = term
        copies = [
            pltpu.make_async_remote_copy(
                src_ref=part.at[which],
                dst_ref=got.at[j],
                send_sem=send.at[j],
                recv_sem=recv.at[j],
                device_id=peer,
                device_id_type=MESH,
            )
            for j, peer in enumerate(peers)
        ]
        for copy in copies:
            copy.start()
        meanwhile()
        for j, copy in enumerate(copies):
            copy.wait_recv()
            term = term + got[j]
        return term, copies

    def drain():
        for offset, zero, cond in around():
            def all_slots(offset=offset, zero=zero):
                for slot in range(CHEB + 1):
                    message(slot, offset, zero).wait_send()
                rows_message(offset).wait_send()

            guarded(cond, all_slots)

    weighed = terms[0][0] * terms[0][1]
    for amount, block in terms[1:]:
        weighed = weighed + amount * block
    term = jnp.sum(weighed, axis=0, keepdims=True)
    term, copies1 = exchanged(term, 0, peers1, got1, send1, recv1, drain)
    term, copies2 = exchanged(term, 1, peers2, got2, send2, recv2, lambda: None)
    answer = jnp.sum(x_mat * term, axis=1, keepdims=True)
    spread = jnp.sum(jnp.where(member, answer, 0.0), axis=0, keepdims=True)
    out[...] = smoothed + weight * spread
    on_lane = lax.broadcasted_iota(jnp.int32, (count, 128), 1)
    on_lane = on_lane == lax.broadcasted_iota(jnp.int32, (count, 128), 0)
    out_c[...] = jnp.sum(jnp.where(on_lane, answer, 0.0), axis=0)[:count]

    for copy in copies1 + copies2:
        copy.wait_send()


def per_device(dims, right_side, coefficient, agg_weight, coarse_factor):
    sizes = right_side.shape
    sx, sy, sz = sizes
    rows = sx * sy
    gx, gy, gz = dims
    flat = [a.reshape(rows, sz) for a in (coefficient, right_side, agg_weight)]
    operands = flat + [coarse_factor] + [jnp.asarray(t) for t in tables(sx, sy, sz)]
    count, unknowns = coarse_factor.shape
    slots = CHEB + 1
    f32 = jnp.float32
    dma = pltpu.SemaphoreType.DMA
    n1, n2 = max(gx * gy - 1, 1), max(gz - 1, 1)
    if gx * gy * gz <= ONE_ROUND:
        n1 = max(gx * gy * gz - 1, 1)
    update, answer = pl.pallas_call(
        functools.partial(kernel, dims, sizes),
        out_shape=[
            pltpu.VMEM((rows, sz), f32),
            pltpu.VMEM((count,), f32),
        ],
        in_specs=[pl.BlockSpec(memory_space=pltpu.HBM)] * len(operands),
        out_specs=[pl.BlockSpec(memory_space=pltpu.VMEM)] * 2,
        scratch_shapes=[pltpu.VMEM(o.shape, o.dtype) for o in operands]
        + [
            pltpu.VMEM((slots, rows, sz), f32),
            pltpu.VMEM((slots, 2, sx, sz), f32),
            pltpu.VMEM((slots, 2, 8, rows), f32),
            pltpu.VMEM((slots, 2, sy, sz), f32),
            pltpu.VMEM((slots, 2, sx, sz), f32),
            pltpu.VMEM((slots, 4, sx, sz), f32),
            pltpu.VMEM((slots, 2, 9, 8, rows), f32),
            pltpu.VMEM((27, count, unknowns), f32),
            pltpu.VMEM((2, 1, unknowns), f32),
            pltpu.VMEM((n1, 1, unknowns), f32),
            pltpu.VMEM((n2, 1, unknowns), f32),
            dma((len(operands),)),
            dma((slots, 27)),
            dma((slots, 27)),
            dma((27,)),
            dma((27,)),
            dma((n1,)),
            dma((n1,)),
            dma((n2,)),
            dma((n2,)),
        ],
        compiler_params=pltpu.CompilerParams(
            collective_id=0, has_side_effects=True, vmem_limit_bytes=63 * 1024 * 1024
        ),
        cost_estimate=pl.CostEstimate(
            flops=400_000_000, bytes_accessed=2_000_000, transcendentals=0
        ),
    )(*operands)
    return update.reshape(sizes), answer


def solution(mesh):
    dims = tuple(mesh.shape[a] for a in ("gx", "gy", "gz"))
    return jax.shard_map(
        functools.partial(per_device, dims),
        mesh=mesh,
        in_specs=(
            P("gx", "gy", "gz"),
            P("gx", "gy", "gz"),
            P("gx", "gy", "gz"),
            P(("gx", "gy", "gz"), None),
        ),
        out_specs=(P("gx", "gy", "gz"), P(("gx", "gy", "gz"))),
        check_vma=False,
    )
```

```python
import functools
import itertools

import jax
import jax.numpy as jnp
import ml_dtypes
import numpy as np
from jax import lax
from jax.experimental import pallas as pl
from jax.experimental.pallas import tpu as pltpu
from jax.sharding import PartitionSpec as P

ORDER = 7
CHEB = 4
MESH = pl.DeviceIdType.MESH
ONE_ROUND = 64
eig_high = 4.0
eig_low = 0.2
gll_inner = np.array(
    [
        -0.8717401485096066,
        -0.5917001814331423,
        -0.20929921790247888,
        0.20929921790247888,
        0.5917001814331423,
        0.8717401485096066,
    ]
)


def legendre_value(nodes, degree):
    previous = nodes * 0.0 + 1.0
    current = nodes
    for step in range(1, degree):
        following = ((2.0 * step + 1.0) * nodes * current - step * previous) / (step + 1.0)
        previous = current
        current = following
    return current


def gll_tables(poly_order):
    point_count = poly_order + 1
    gll_nodes = np.concatenate([np.array([-1.0]), gll_inner, np.array([1.0])])
    at_nodes = legendre_value(gll_nodes, poly_order)
    weights = 2.0 / (poly_order * point_count * at_nodes**2)
    differences = gll_nodes[:, None] - gll_nodes[None, :] + np.eye(point_count)
    derivative = at_nodes[:, None] / (at_nodes[None, :] * differences) * (1.0 - np.eye(point_count))
    end_value = poly_order * point_count / 4.0
    end_row = np.concatenate(
        [np.array([-end_value]), np.zeros(poly_order - 1), np.array([end_value])]
    )
    derivative = derivative + np.eye(point_count) * end_row[None, :]
    return (derivative, weights)


def halves(matrix):
    full = np.asarray(matrix, np.float32)
    high = full.astype(ml_dtypes.bfloat16)
    low = (full - high.astype(np.float32)).astype(ml_dtypes.bfloat16)
    return np.stack([high, low])


def tables(size_x, size_y, size_z):
    points = ORDER + 1
    derivative, weights = gll_tables(ORDER)
    derivative = derivative.astype(np.float32)
    squared = derivative * derivative
    ex, ey, ez = size_x // points, size_y // points, size_z // points

    def along_x(m):
        return np.kron(np.kron(np.eye(ex), m), np.eye(size_y))

    def along_y(m):
        return np.kron(np.eye(size_x), np.kron(np.eye(ey), m))

    def along_z(m):
        return np.kron(np.eye(ez), m)

    forward = np.concatenate([along_x(derivative), along_y(derivative)], axis=0)
    weights = weights.astype(np.float32)
    w_xy = np.kron(np.tile(weights, ex), np.tile(weights, ey))
    quad = (w_xy[:, None] * np.tile(weights, ez)[None, :]).astype(np.float32)
    return (
        quad,
        halves(along_x(squared.T) + along_y(squared.T)),
        halves(along_z(squared)),
        halves(forward),
        halves(along_z(derivative.T)),
        halves(forward.T),
        halves(along_z(derivative)),
    )


def split(value):
    high = value.astype(jnp.bfloat16)
    low = (value - high.astype(jnp.float32)).astype(jnp.bfloat16)
    return high, low


def dot(a, b):
    return jnp.dot(a, b, preferred_element_type=jnp.float32)


def from_left(mat, value):
    high, low = split(value)
    size = mat.shape[1]
    both = dot(jnp.concatenate([mat[0], mat[1]], axis=0), high)
    return both[:size] + (both[size:] + dot(mat[0], low))


def from_right(value, mat):
    high, low = split(value)
    size = value.shape[0]
    both = dot(jnp.concatenate([high, low], axis=0), mat[0])
    return both[:size] + (both[size:] + dot(high, mat[1]))


def kernel(dims, sizes, *refs):
    gx, gy, gz = dims
    sx, sy, sz = sizes
    rows = sx * sy
    inputs, (out, out_c), scratch = refs[:11], refs[11:13], refs[13:]
    held, (field, yface, zface, xr, yr, er, zr, xn, part, got1, got2), sems = (
        scratch[:11],
        scratch[11:22],
        scratch[22:],
    )
    in_sem, send_sem, recv_sem, sendx, recvx, send1, recv1, send2, recv2 = sems
    ix, iy, iz = (lax.axis_index(a) for a in ("gx", "gy", "gz"))

    loads = [pltpu.make_async_copy(i, h, in_sem.at[k]) for k, (i, h) in enumerate(zip(inputs, held))]
    coef, rhs, agg, factor, quad, sq_xy, sq_z, f_xy, f_z, b_xy, b_z = held

    for buf in (xr, yr, er, zr, xn):
        buf[...] = jnp.zeros_like(buf)

    def options(index, count):
        if count == 1:
            return [(0, None)]
        if count == 2:
            return [(0, None), (1 - 2 * index, None)]
        return [(0, None), (1, index < count - 1), (-1, index > 0)]

    def around():
        every = itertools.product(options(ix, gx), options(iy, gy), options(iz, gz))

        def near(one):
            return sum(isinstance(d, int) and d == 0 for d, _ in one)

        for (dx, cx), (dy, cy), (dz, cz) in sorted(every, key=near):
            zero = [isinstance(d, int) and d == 0 for d in (dx, dy, dz)]
            if all(zero):
                continue
            conds = [c for c in (cx, cy, cz) if c is not None]
            cond = None
            for c in conds:
                cond = c if cond is None else jnp.logical_and(cond, c)
            yield (dx, dy, dz), zero, cond

    def guarded(cond, action):
        if cond is None:
            action()
        else:
            pl.when(cond)(action)

    nxy = gx * gy
    me_xy = ix * gy + iy
    one_round = nxy * gz <= ONE_ROUND
    peers1 = []
    if one_round:
        for j in range(1, nxy * gz):
            other = lax.rem(me_xy * gz + iz + j, nxy * gz)
            peers1.append((other // (gy * gz), lax.rem(other // gz, gy), lax.rem(other, gz)))
        peers2 = []
    else:
        for j in range(1, nxy):
            other = lax.rem(me_xy + j, nxy)
            peers1.append((other // gy, lax.rem(other, gy), iz))
        peers2 = [(ix, iy, lax.rem(iz + j, gz)) for j in range(1, gz)]

    barrier = pltpu.get_barrier_semaphore()
    for offset, _, cond in [] if one_round else around():
        def greet(offset=offset):
            pl.semaphore_signal(
                barrier,
                inc=1,
                device_id=(ix + offset[0], iy + offset[1], iz + offset[2]),
                device_id_type=MESH,
            )

        guarded(cond, greet)
    for peer in peers1 + peers2:
        pl.semaphore_signal(barrier, inc=1, device_id=peer, device_id_type=MESH)

    for k in (0, 6, 4, 5, 2, 3, 1, 7, 8, 9, 10):
        loads[k].start()

    def present(index, count):
        if count <= 2:
            return count
        return 3 - (index == 0).astype(jnp.int32) - (index == count - 1).astype(jnp.int32)

    greeted = len(peers1) + len(peers2)
    if not one_round:
        greeted = greeted + present(ix, gx) * present(iy, gy) * present(iz, gz) - 1

    def message(slot, offset, zero):
        dx, dy, dz = offset
        mark = (1 - dx) * 9 + (1 - dy) * 3 + (1 - dz)
        low_x, low_y, low_z = [(1 + d) // 2 for d in offset]
        if not zero[2]:
            src = zface.at[slot, low_z]
            dst = zr.at[slot, 1 - low_z, (1 - dx) * 3 + (1 - dy)]
        elif not zero[1] and not zero[0]:
            src = yface.at[slot, low_y]
            dst = er.at[slot, (1 - low_x) * 2 + (1 - low_y)]
        elif not zero[1]:
            src = yface.at[slot, low_y]
            dst = yr.at[slot, 1 - low_y]
        else:
            src = field.at[slot, pl.ds(pl.multiple_of(low_x * (rows - sy), sy), sy)]
            dst = xr.at[slot, 1 - low_x]
        return pltpu.make_async_remote_copy(
            src_ref=src,
            dst_ref=dst,
            send_sem=send_sem.at[slot, mark],
            recv_sem=recv_sem.at[slot, mark],
            device_id=(ix + dx, iy + dy, iz + dz),
            device_id_type=MESH,
        )

    def incoming(slot, offset, zero):
        return message(slot, tuple(-d for d in offset), zero)

    def rows_message(offset):
        dx, dy, dz = offset
        mark = (1 - dx) * 9 + (1 - dy) * 3 + (1 - dz)
        return pltpu.make_async_remote_copy(
            src_ref=factor,
            dst_ref=xn.at[mark],
            send_sem=sendx.at[mark],
            recv_sem=recvx.at[mark],
            device_id=(ix + dx, iy + dy, iz + dz),
            device_id_type=MESH,
        )

    row = lax.broadcasted_iota(jnp.int32, (rows, sz), 0)
    lane = lax.broadcasted_iota(jnp.int32, (rows, sz), 1)
    y_at = lax.rem(row, sy)
    y_node = lax.rem(row, 8)
    z_node = lax.rem(lane, 8)
    x_of = lax.broadcasted_iota(jnp.int32, (sx, sz), 0)
    p_lane = lax.broadcasted_iota(jnp.int32, (8, rows), 1)
    p_y = lax.rem(p_lane, sy)
    lane_half = lax.broadcasted_iota(jnp.int32, (rows, 128), 1)

    def plane(slot, side):
        def summed_x(b):
            own = zr[slot, side, 3 + b]
            low = jnp.where(p_lane < sy, pltpu.roll(zr[slot, side, b], sy, 1), 0.0)
            high = jnp.where(
                p_lane >= rows - sy, pltpu.roll(zr[slot, side, 6 + b], rows - sy, 1), 0.0
            )
            return own + low + high

        before, mine, after = summed_x(0), summed_x(1), summed_x(2)
        low = jnp.where(
            p_y == 0, pltpu.roll(before, rows - (sy - 1), 1), pltpu.roll(mine, 1, 1)
        )
        high = jnp.where(
            p_y == sy - 1, pltpu.roll(after, sy - 1, 1), pltpu.roll(mine, rows - 1, 1)
        )
        node = lax.rem(p_lane, 8)
        return mine + jnp.where(node == 0, low, 0.0) + jnp.where(node == 7, high, 0.0)

    def end_rows(local):
        return jnp.where(lane_half < 64, local[:, :128], local[:, sz - 128 :]).T

    def publish(slot, local):
        field[slot] = local
        cube = local.reshape(sx, sy, sz)
        yface[slot, 0] = cube[:, 0, :]
        yface[slot, 1] = cube[:, sy - 1, :]
        turned = end_rows(local)
        zface[slot, 0] = turned[:8]
        zface[slot, 1] = turned[120:]
        if slot == 0:
            pl.semaphore_wait(barrier, greeted)
        for offset, zero, cond in around():
            guarded(cond, lambda: message(slot, offset, zero).start())

    def assemble(slot, local, meanwhile):
        publish(slot, local)
        meanwhile()
        for offset, zero, cond in around():
            guarded(cond, lambda: incoming(slot, offset, zero).wait_recv())
        value = jnp.concatenate(
            [local[:sy] + xr[slot, 0], local[sy : rows - sy], local[rows - sy :] + xr[slot, 1]],
            axis=0,
        )

        def y_side(side):
            face = yr[slot, side]
            face = face + jnp.where(x_of == 0, jnp.broadcast_to(er[slot, side][sx - 1 :], (sx, sz)), 0.0)
            face = face + jnp.where(x_of == sx - 1, jnp.broadcast_to(er[slot, 2 + side][:1], (sx, sz)), 0.0)
            return jnp.broadcast_to(face[:, None, :], (sx, sy, sz)).reshape(rows, sz)

        low = jnp.where(y_at == 0, y_side(0), pltpu.roll(value, 1, 0))
        high = jnp.where(y_at == sy - 1, y_side(1), pltpu.roll(value, rows - 1, 0))
        value = value + jnp.where(y_node == 0, low, 0.0) + jnp.where(y_node == 7, high, 0.0)
        z_low = plane(slot, 0)[7:]
        z_high = plane(slot, 1)[:1]
        ends = jnp.concatenate(
            [jnp.broadcast_to(z_low, (64, rows)), jnp.broadcast_to(z_high, (64, rows))], axis=0
        ).T
        ends = jnp.concatenate([ends] * (sz // 128), axis=1)
        low = jnp.where(lane == 0, ends, pltpu.roll(value, 1, 1))
        high = jnp.where(lane == sz - 1, ends, pltpu.roll(value, sz - 1, 1))
        return value + jnp.where(z_node == 0, low, 0.0) + jnp.where(z_node == 7, high, 0.0)

    def wait_load(*which):
        for k in which:
            loads[k].wait()

    def early():
        wait_load(2, 3)
        publish(CHEB, agg[...])
        wait_load(1, 7, 8, 9, 10)

    def spread_rows():
        for offset, zero, cond in around():
            guarded(cond, lambda: rows_message(offset).start())

    def arrived():
        for offset, zero, cond in around():
            def both(offset=offset, zero=zero):
                incoming(CHEB, offset, zero).wait_recv()
                rows_message(tuple(-d for d in offset)).wait_recv()

            guarded(cond, both)

    wait_load(0, 4, 5, 6)
    scaled = coef[...] * quad[...]
    diagonal = assemble(0, from_left(sq_xy, scaled) + from_right(scaled, sq_z), early)
    inverse = 1.0 / diagonal
    theta = (eig_high + eig_low) / 2.0
    delta = (eig_high - eig_low) / 2.0
    sigma = theta / delta
    residual = rhs[...]
    direction = inverse * residual * (1.0 / theta)
    smoothed = direction
    rho = 1.0 / sigma
    for sweep in range(CHEB):
        grads = from_left(f_xy, direction)
        grad_z = from_right(direction, f_z)
        flux = jnp.concatenate([scaled * grads[:rows], scaled * grads[rows:]], axis=0)
        local = from_left(b_xy, flux) + from_right(scaled * grad_z, b_z)
        if sweep + 1 < CHEB:
            meanwhile = arrived if sweep + 2 == CHEB else spread_rows if sweep == 0 else lambda: None
            residual = residual - assemble(sweep + 1, local, meanwhile)
            rho_new = 1.0 / (2.0 * sigma - rho)
            direction = rho_new * rho * direction + (2.0 * rho_new / delta) * inverse * residual
            smoothed = smoothed + direction
            rho = rho_new

    weight = agg[...]
    count, unknowns = factor.shape
    member = lax.broadcasted_iota(jnp.int32, (count, sz), 1) // (sz // count)
    member = member == lax.broadcasted_iota(jnp.int32, (count, sz), 0)
    last = CHEB

    def per_aggregate(column):
        return jnp.sum(jnp.where(member, column, 0.0), axis=1, keepdims=True)

    def inner_y(value, at, axis):
        size = value.shape[axis]
        node = lax.rem(at, 8)
        low = jnp.where((node == 0) & (at != 0), pltpu.roll(value, 1, axis), 0.0)
        high = jnp.where((node == 7) & (at != sy - 1), pltpu.roll(value, size - 1, axis), 0.0)
        return value + low + high

    low = jnp.where((z_node == 0) & (lane != 0), pltpu.roll(local, 1, 1), 0.0)
    high = jnp.where((z_node == 7) & (lane != sz - 1), pltpu.roll(local, sz - 1, 1), 0.0)
    joined = local + low + high
    cube = joined.reshape(sx, sy, sz)
    y_ends = (cube[:, 0, :], cube[:, sy - 1, :])

    def total(value):
        return jnp.sum(value, axis=0, keepdims=True)

    terms = [
        (per_aggregate(total(weight * residual - inner_y(weight, y_at, 0) * joined)), factor[...])
    ]
    for side in range(2):
        layer = inner_y(xr[last, side], y_at[:sy], 0)
        own = joined[side * (rows - sy) : side * (rows - sy) + sy]
        terms.append((-per_aggregate(total(layer * own)), xn[side * 18 + 4]))
        terms.append((-per_aggregate(total(yr[last, side] * y_ends[side])), xn[9 + side * 6 + 1]))
        for other in range(2):
            line = er[last, side * 2 + other][(1 - side) * (sx - 1) : (1 - side) * (sx - 1) + 1]
            own = y_ends[other][side * (sx - 1) : side * (sx - 1) + 1]
            terms.append((-per_aggregate(line * own), xn[side * 18 + other * 6 + 1]))

    turned = end_rows(local)
    tile_row = lax.broadcasted_iota(jnp.int32, (8, 1), 0)
    for side in range(2):
        own = jnp.broadcast_to(turned[side * 127 : side * 127 + 1], (8, rows))
        for a, b in itertools.product(range(3), range(3)):
            face = zr[last, side, a * 3 + b]
            if a == 0:
                face = jnp.where(p_lane < sy, pltpu.roll(face, sy, 1), 0.0)
            elif a == 2:
                face = jnp.where(p_lane >= rows - sy, pltpu.roll(face, rows - sy, 1), 0.0)
            if b == 0:
                face = jnp.where(p_y == 0, pltpu.roll(face, rows - (sy - 1), 1), 0.0)
            elif b == 2:
                face = jnp.where(p_y == sy - 1, pltpu.roll(face, sy - 1, 1), 0.0)
            else:
                face = inner_y(face, p_y, 1)
            amount = jnp.sum(face * own, axis=1, keepdims=True)
            amount = jnp.where(tile_row == 7 * (1 - side), amount, 0.0)
            terms.append((-amount, xn[a * 9 + b * 3 + side * 2]))
    x_mat = factor[...]

    def exchanged(term, which, peers, got, send, recv, meanwhile):
        part[which] = term
        copies = [
            pltpu.make_async_remote_copy(
                src_ref=part.at[which],
                dst_ref=got.at[j],
                send_sem=send.at[j],
                recv_sem=recv.at[j],
                device_id=peer,
                device_id_type=MESH,
            )
            for j, peer in enumerate(peers)
        ]
        for copy in copies:
            copy.start()
        meanwhile()
        for j, copy in enumerate(copies):
            copy.wait_recv()
            term = term + got[j]
        return term, copies

    def drain():
        for offset, zero, cond in around():
            def all_slots(offset=offset, zero=zero):
                for slot in range(CHEB + 1):
                    message(slot, offset, zero).wait_send()
                rows_message(offset).wait_send()

            guarded(cond, all_slots)

    weighed = terms[0][0] * terms[0][1]
    for amount, block in terms[1:]:
        weighed = weighed + amount * block
    term = jnp.sum(weighed, axis=0, keepdims=True)
    term, copies1 = exchanged(term, 0, peers1, got1, send1, recv1, drain)
    term, copies2 = exchanged(term, 1, peers2, got2, send2, recv2, lambda: None)
    answer = jnp.sum(x_mat * term, axis=1, keepdims=True)
    spread = jnp.sum(jnp.where(member, answer, 0.0), axis=0, keepdims=True)
    out[...] = smoothed + weight * spread
    on_lane = lax.broadcasted_iota(jnp.int32, (count, 128), 1)
    on_lane = on_lane == lax.broadcasted_iota(jnp.int32, (count, 128), 0)
    out_c[...] = jnp.sum(jnp.where(on_lane, answer, 0.0), axis=0)[:count]

    for copy in copies1 + copies2:
        copy.wait_send()


def per_device(dims, right_side, coefficient, agg_weight, coarse_factor):
    sizes = right_side.shape
    sx, sy, sz = sizes
    rows = sx * sy
    gx, gy, gz = dims
    flat = [a.reshape(rows, sz) for a in (coefficient, right_side, agg_weight)]
    operands = flat + [coarse_factor] + [jnp.asarray(t) for t in tables(sx, sy, sz)]
    count, unknowns = coarse_factor.shape
    slots = CHEB + 1
    f32 = jnp.float32
    dma = pltpu.SemaphoreType.DMA
    n1, n2 = max(gx * gy - 1, 1), max(gz - 1, 1)
    if gx * gy * gz <= ONE_ROUND:
        n1 = max(gx * gy * gz - 1, 1)
    update, answer = pl.pallas_call(
        functools.partial(kernel, dims, sizes),
        out_shape=[
            pltpu.VMEM((rows, sz), f32),
            pltpu.VMEM((count,), f32),
        ],
        in_specs=[pl.BlockSpec(memory_space=pltpu.HBM)] * len(operands),
        out_specs=[pl.BlockSpec(memory_space=pltpu.VMEM)] * 2,
        scratch_shapes=[pltpu.VMEM(o.shape, o.dtype) for o in operands]
        + [
            pltpu.VMEM((slots, rows, sz), f32),
            pltpu.VMEM((slots, 2, sx, sz), f32),
            pltpu.VMEM((slots, 2, 8, rows), f32),
            pltpu.VMEM((slots, 2, sy, sz), f32),
            pltpu.VMEM((slots, 2, sx, sz), f32),
            pltpu.VMEM((slots, 4, sx, sz), f32),
            pltpu.VMEM((slots, 2, 9, 8, rows), f32),
            pltpu.VMEM((27, count, unknowns), f32),
            pltpu.VMEM((2, 1, unknowns), f32),
            pltpu.VMEM((n1, 1, unknowns), f32),
            pltpu.VMEM((n2, 1, unknowns), f32),
            dma((len(operands),)),
            dma((slots, 27)),
            dma((slots, 27)),
            dma((27,)),
            dma((27,)),
            dma((n1,)),
            dma((n1,)),
            dma((n2,)),
            dma((n2,)),
        ],
        compiler_params=pltpu.CompilerParams(
            collective_id=0, has_side_effects=True, vmem_limit_bytes=63 * 1024 * 1024
        ),
        cost_estimate=pl.CostEstimate(
            flops=400_000_000, bytes_accessed=2_000_000, transcendentals=0
        ),
    )(*operands)
    return update.reshape(sizes), answer


def solution(mesh):
    dims = tuple(mesh.shape[a] for a in ("gx", "gy", "gz"))
    return jax.shard_map(
        functools.partial(per_device, dims),
        mesh=mesh,
        in_specs=(
            P("gx", "gy", "gz"),
            P("gx", "gy", "gz"),
            P("gx", "gy", "gz"),
            P(("gx", "gy", "gz"), None),
        ),
        out_specs=(P("gx", "gy", "gz"), P(("gx", "gy", "gz"))),
        check_vma=False,
    )
```
